512 devices in a mesh: blk: 16 (over z_lo, core), rows: 32 (over y, x, z_hi).
Axes of the slice: x: 4, y: 4, z: 16 (z_hi: 2, z_lo: 8; z = z_hi * 8 + z_lo), core: 2. Of those that a mesh axis runs over, the one named last changes fastest.
Arguments:
- p_vals: bfloat16 [64, 64, 8, 128, 128], P('blk', 'rows'), may hold values from -2.5 to 2.5
- p_cols: int32 [64, 64, 8], replicated, may hold values from 0 to 4095, as said below
- c_cols: int32 [64, 64, 12], P('blk', 'rows'), may hold values from 0 to 4095, as said below
Outputs:
- c_vals: bfloat16 [64, 64, 12, 128, 128], P('blk', 'rows')
The draws below stay inside these ranges and needn't reach their ends.
Inputs may be any that keep to these rules, and one draw needn't show every extreme that they name: `p_cols`: each block row's 8 columns are distinct, the row's own site among them, and each lies within one site of the row's site along both lattice dimensions, cyclically. `c_cols`: each block row's 12 pattern columns are distinct, the row's own site among them, and each lies within two sites of the row's site along both lattice dimensions, cyclically.
All inputs are finite; a program needn't handle non-finite values.
Results may differ from the reference program's by a relative error of at most 0.001.
Values may be sent and summed in bfloat16 or wider, within the bound.
No kernel may reach another device: no remote copies, remote signals or barrier semaphores. Data moves between devices by JAX's collectives and lax.ppermute only.
A program may use at most 64 MiB of HBM per device.

```python
import jax
import jax.numpy as jnp
import numpy as np
from jax import lax

B = 128
K = 8
NC = 12
NX = 64
NY = 64


def stencil_pick(key, reach_cells, count):
    side = 2 * reach_cells + 1
    code_list = np.array([c for c in range(side * side) if c != reach_cells * side + reach_cells], np.int32)
    step_x = jnp.asarray(code_list // side - reach_cells)
    step_y = jnp.asarray(code_list % side - reach_cells)
    key_list = jax.random.split(key, NX * NY)
    chosen = jax.vmap(lambda one_key: jax.random.permutation(one_key, code_list.shape[0]))(key_list)[:, :count - 1]
    cell_ids = jnp.arange(NX * NY, dtype=jnp.int32)
    home_x = cell_ids // NY
    home_y = cell_ids % NY
    near_x = (home_x[:, None] + step_x[chosen]) % NX
    near_y = (home_y[:, None] + step_y[chosen]) % NY
    others = (near_x * NY + near_y).astype(jnp.int32)
    return jnp.concatenate([cell_ids[:, None], others], axis=1).reshape(NX, NY, count)


def draw_p_cols(key, part):
    key = jax.random.fold_in(key, 1)
    return stencil_pick(key, 1, K)


def draw_c_cols(key, part):
    key = jax.random.fold_in(key, 2)
    return stencil_pick(key, 2, NC)


def levels(stream_key, dims, cuts, low, largest):
    loudness, own = 1.0, jax.random.fold_in(stream_key, 6)
    for axis_at, blocks in cuts:
        heights = jnp.exp(jax.random.uniform(jax.random.fold_in(own, axis_at), (blocks,), jnp.float32, low / len(cuts), largest / len(cuts)))
        loudness = loudness * jnp.repeat(heights, dims[axis_at] // blocks).reshape([-1 if axis == axis_at else 1 for axis in range(len(dims))])
    return loudness


def centred(key, extent, width, limit, shards=(), held_as=jnp.bfloat16):
    drawn = jax.random.normal(key, extent, jnp.float32) * width
    if len(shards) > 0:
        drawn = levels(key, extent, shards, -0.22, 0.18) * drawn
    return jnp.clip(drawn, min=-limit, max=limit).astype(held_as)


def setup_inputs(seed: int = 0) -> dict:
    streams_of = jax.random.split(jax.random.key(seed), 4)
    return {
        "p_vals": centred(streams_of[0], (NX, NY, K, B, B), ((B * K) ** -0.25), 2.5, ((0, 16), (1, 32))),
        "p_cols": draw_p_cols(jax.random.fold_in(streams_of[3], 71), 0),
        "c_cols": draw_c_cols(jax.random.fold_in(streams_of[3], 71), 0),
    }


def contract_rows(left_blocks, right_blocks, right_cols, targets):
    hits = (right_cols[:, None, :, :] == targets[:, :, None, None]).astype(jnp.int32)
    which = jnp.argmax(hits, axis=3).astype(jnp.int32)
    present = jnp.max(hits, axis=3) > 0
    picked = jnp.take_along_axis(right_blocks[:, None], which[:, :, :, None, None, None], axis=3)[:, :, :, 0]
    picked = jnp.where(present[:, :, :, None, None], picked, jnp.zeros_like(picked))
    merged = jnp.einsum("ymab,ynmbc->ynac", left_blocks.astype(jnp.float32), picked.astype(jnp.float32))
    return merged.astype(jnp.bfloat16)


def reference(p_vals, p_cols, c_cols):
    stacked = p_vals.reshape(NX * NY, K, B, B)
    col_table = p_cols.reshape(NX * NY, K)

    def one_column(column):
        left_blocks = lax.dynamic_index_in_dim(p_vals, column, 0, False)
        partners = lax.dynamic_index_in_dim(p_cols, column, 0, False)
        targets = lax.dynamic_index_in_dim(c_cols, column, 0, False)
        return contract_rows(left_blocks, stacked[partners], col_table[partners], targets)

    return lax.map(one_column, jnp.arange(NX, dtype=jnp.int32))
```

```python
import jax
import jax.numpy as jnp
import numpy as np
from jax import lax
from jax.experimental import pallas as pl
from jax.experimental.pallas import tpu as pltpu
from jax.sharding import PartitionSpec as P

AXES = ("blk", "rows")
OWN, EARLY_LOW, EARLY_HIGH, EARLY_WRAP, SIDE_LOW, SIDE_HIGH, LATE_LOW, LATE_HIGH, LATE_WRAP, PIECES = (
    0, 8, 10, 12, 13, 17, 21, 23, 25, 26
)


def send(value, moves, n_rows):
    return lax.ppermute(value, AXES, [(a[0] * n_rows + a[1], b[0] * n_rows + b[1]) for a, b in moves])


def moves_y(shift, n_blk, n_rows):
    return [((b, r), (b, (r + shift) % n_rows)) for b in range(n_blk) for r in range(n_rows)]


def moves_x(shift, n_blk, n_rows):
    moves = []
    for b in range(n_blk):
        for r in range(n_rows):
            inside = 0 <= b + shift < n_blk
            moves.append(((b, r), ((b + shift) % n_blk, r if inside else (r + 1) % n_rows)))
    return moves


def moves_wrap(n_blk, n_rows):
    edges = ((n_blk - 1, 0), (0, n_blk - 1))
    return [((b, r), (to, (r - 1) % n_rows)) for b, to in edges for r in range(n_rows)]


def accumulate(table_m, table_q, own, x, col, pieces, write, unroll):
    site = x * 2 + col
    left = jnp.concatenate([own[x, col, table_m[site * PIECES + number]] for number, _ in pieces], axis=1)

    def pair(h, carry):
        halves = []
        for n in (2 * h, 2 * h + 1):
            rows = []
            for number, block_of in pieces:
                q = table_q[(site * PIECES + number) * 12 + n]
                block = block_of(jnp.minimum(q, 7))
                rows.append(jnp.where(q < 8, block, jnp.zeros_like(block)))
            halves.append(jnp.concatenate(rows, axis=0))
        right = jnp.concatenate(halves, axis=1)
        total = jnp.dot(left, right, preferred_element_type=jnp.float32)
        write(x, col, 2 * h, total[:, :128])
        write(x, col, 2 * h + 1, total[:, 128:])
        return carry

    lax.fori_loop(0, 6, pair, 0, unroll=unroll)


def block_from(ref, *lead):
    return lambda q: ref[(*lead, q)]


def first_kernel(table_m, table_q, own, up, down, wrap, acc):
    cells_x = own.shape[0]

    def write(x, col, n, total):
        acc[x, col, n] = total

    for x in range(cells_x):
        for col in range(2):
            pieces = []
            for near in (x - 1, x, x + 1):
                if near < 0:
                    pieces += [(EARLY_LOW + y, block_from(up, y)) for y in range(2)]
                elif near >= cells_x:
                    pieces += [(EARLY_HIGH + y, block_from(down, y)) for y in range(2)]
                else:
                    pieces += [(OWN + near * 2 + y, block_from(own, near, y)) for y in range(2)]
            if x in (0, cells_x - 1):
                pieces.append((EARLY_WRAP, block_from(wrap)))
            accumulate(table_m, table_q, own, x, col, pieces, write, 2)


def rim_kernel(table_m, table_q, own, acc, rim_low, rim_high, out):
    cells_x = own.shape[0]
    rims = (rim_low, rim_high)

    def write(x, col, n, total):
        out[x, col, n] = acc[x, col, n] + total

    for x in range(cells_x):
        for col in range(2):
            at = int(x >= cells_x // 2)
            number = (SIDE_LOW, SIDE_HIGH)[col] + at * (cells_x - 1)
            accumulate(table_m, table_q, own, x, col, [(number, block_from(rims[col], at))], write, 2)


def last_kernel(table_m, table_q, own, acc, mid_low, mid_high, up, down, wrap, out, held, sems):
    cells_x = own.shape[0]
    mids = (mid_low, mid_high)

    def write(x, col, n, total):
        held[x, col, n] = (acc[x, col, n] + total).astype(jnp.bfloat16)

    copies = []
    for x in (1, 2, 0, 3):
        for col in range(2):
            first = (SIDE_LOW, SIDE_HIGH)[col]
            pieces = [
                (first + near, block_from(mids[col], near - 1))
                for near in (x - 1, x, x + 1)
                if 0 < near < cells_x - 1
            ]
            if x == 0:
                pieces += [(LATE_LOW + y, block_from(up, y)) for y in range(2)]
            if x == cells_x - 1:
                pieces += [(LATE_HIGH + y, block_from(down, y)) for y in range(2)]
            if x in (0, cells_x - 1):
                pieces.append((LATE_WRAP, block_from(wrap)))
            accumulate(table_m, table_q, own, x, col, pieces, write, 6)
            copies.append(pltpu.make_async_copy(held.at[x, col], out.at[x, col], sems.at[x, col]))
            copies[-1].start()
    for copy in copies:
        copy.wait()


def run_kernel(body, tables, own, sites, flops, last=False):
    shape = (own.shape[0], 2, 12, 128, 128)
    return pl.pallas_call(
        body,
        out_shape=jax.ShapeDtypeStruct(shape, jnp.bfloat16 if last else jnp.float32),
        in_specs=[pl.BlockSpec(memory_space=pltpu.SMEM)] * 2
        + [pl.BlockSpec(memory_space=pltpu.VMEM)] * (1 + len(sites)),
        out_specs=pl.BlockSpec(memory_space=pl.ANY if last else pltpu.VMEM),
        scratch_shapes=[pltpu.VMEM(shape, jnp.bfloat16), pltpu.SemaphoreType.DMA(shape[:2])] if last else [],
        compiler_params=pltpu.CompilerParams(vmem_limit_bytes=32 * 2**20),
        cost_estimate=pl.CostEstimate(flops=flops, bytes_accessed=2**10, transcendentals=0),
    )(*tables, own, *sites)


def make_tables(p_cols, c_cols, cells_x, cells_y):
    total_x, total_y, blocks = p_cols.shape
    at_blk, at_row = lax.axis_index("blk"), lax.axis_index("rows")
    first, last = at_blk == 0, at_blk == lax.axis_size("blk") - 1
    near = [(x, y) for x in range(cells_x) for y in range(cells_y)]
    wide = [-1, -1, cells_x, cells_x]
    sides, side_y = list(range(cells_x)) * 2, [-1] * cells_x + [cells_y] * cells_x
    dx = [x for x, _ in near] + wide + [0] + sides + wide + [0]
    plain = [y for _, y in near] + [0, 1] * 2 + [2] + side_y + [-1, 2] * 2 + [1]
    turned = [y for _, y in near] + [-2, -1] * 2 + [2] + side_y + [-3, 0] * 2 + [1]
    dx, plain, turned = (np.array(v, np.int32) for v in (dx, plain, turned))
    numbers = np.arange(PIECES)
    is_wrap = (numbers == EARLY_WRAP) | (numbers == LATE_WRAP)
    dx = jnp.where(is_wrap, jnp.where(first, -1, cells_x), dx)
    swapped = ((dx < 0) & first) | ((dx >= cells_x) & last)
    dy = jnp.where(swapped, turned, plain)
    site_x = (at_blk * cells_x + dx + total_x) % total_x
    site_y = (at_row * cells_y + dy + total_y) % total_y
    ids = site_x * total_y + site_y
    cols = p_cols.reshape(total_x * total_y, blocks)[ids]
    ids = jnp.where(is_wrap & ~(first | last), -1, ids)
    own = cols[: cells_x * cells_y]
    slots = jnp.arange(blocks, dtype=jnp.int32)
    is_left = own[:, None, :] == ids[None, :, None]
    table_m = jnp.sum(jnp.where(is_left, slots, 0), axis=2)
    has_left = jnp.any(is_left, axis=2)
    targets = c_cols.reshape(cells_x * cells_y, -1)
    is_right = (cols[None, :, None, :] == targets[:, None, :, None]) & has_left[:, :, None, None]
    table_q = 8 + jnp.sum(jnp.where(is_right, slots - 8, 0), axis=3)
    return table_m.reshape(-1).astype(jnp.int32), table_q.reshape(-1).astype(jnp.int32)


def on_device(p_vals, p_cols, c_cols):
    cells_x, cells_y = p_vals.shape[:2]
    n_blk, n_rows = lax.axis_size("blk"), lax.axis_size("rows")
    last = cells_x - 1
    first = lax.axis_index("blk") == 0
    along_y = lambda value, shift: send(value, moves_y(shift, n_blk, n_rows), n_rows)
    along_x = lambda value, shift: send(value, moves_x(shift, n_blk, n_rows), n_rows)
    past_edge = lambda value: send(value, moves_wrap(n_blk, n_rows), n_rows)
    tie = lax.optimization_barrier

    rim_low = along_y(jnp.stack([p_vals[0, 1], p_vals[last, 1]]), 1)
    rim_high = along_y(jnp.stack([p_vals[0, 0], p_vals[last, 0]]), -1)

    edges, p_cols, c_cols = tie(((p_vals[last], p_vals[0]), p_cols, c_cols))
    tables = make_tables(p_cols, c_cols, cells_x, cells_y)
    single = jnp.where(first, edges[1][0], edges[0][0])
    early = [along_x(edges[0], 1), along_x(edges[1], -1), past_edge(single)]

    early, middle = tie((early, (p_vals[1:last, 1], p_vals[1:last, 0])))
    mid_low = along_y(middle[0], 1)
    mid_high = along_y(middle[1], -1)

    acc = run_kernel(first_kernel, tables, p_vals, early, 4 * 10**9)
    acc, rim_low, rim_high = tie((acc, rim_low, rim_high))
    single = jnp.where(first, rim_low[0], rim_low[1])
    late = [
        along_x(jnp.stack([rim_low[1], rim_high[1]]), 1),
        along_x(jnp.stack([rim_low[0], rim_high[0]]), -1),
        past_edge(single),
    ]
    acc = run_kernel(rim_kernel, tables, p_vals, [acc, rim_low, rim_high], 10**6)
    return run_kernel(last_kernel, tables, p_vals, [acc, mid_low, mid_high, *late], 10**6, last=True)


def solution(mesh):
    placed = (P("blk", "rows", None, None, None), P(), P("blk", "rows", None))
    return jax.shard_map(
        on_device,
        mesh=mesh,
        in_specs=placed,
        out_specs=P("blk", "rows", None, None, None),
        check_vma=False,
    )
```

```python
import jax
import jax.numpy as jnp
import numpy as np
from jax import lax
from jax.experimental import pallas as pl
from jax.experimental.pallas import tpu as pltpu
from jax.sharding import PartitionSpec as P

AXES = ("blk", "rows")
OWN, SIDE_LOW, SIDE_HIGH, NEAR_LOW, NEAR_HIGH, WRAP, PIECES = 0, 8, 12, 16, 20, 24, 26
BLOCKS = (12, 128, 128)


def send(value, moves, n_rows):
    return lax.ppermute(value, AXES, [(a[0] * n_rows + a[1], b[0] * n_rows + b[1]) for a, b in moves])


def moves_y(shift, n_blk, n_rows):
    return [((b, r), (b, (r + shift) % n_rows)) for b in range(n_blk) for r in range(n_rows)]


def moves_x(shift, n_blk, n_rows):
    moves = []
    for b in range(n_blk):
        for r in range(n_rows):
            inside = 0 <= b + shift < n_blk
            moves.append(((b, r), ((b + shift) % n_blk, r if inside else (r + 1) % n_rows)))
    return moves


def moves_wrap(n_blk, n_rows):
    edges = ((n_blk - 1, 0), (0, n_blk - 1))
    return [((b, r), (to, (r - 1) % n_rows)) for b, to in edges for r in range(n_rows)]


def accumulate(table_m, table_q, own, x, col, pieces, write, unroll):
    site = x * 2 + col
    left = jnp.concatenate([own[x, col, table_m[site * PIECES + number]] for number, _ in pieces], axis=1)

    def pair(h, carry):
        halves = []
        for n in (2 * h, 2 * h + 1):
            rows = []
            for number, block_of in pieces:
                q = table_q[(site * PIECES + number) * 12 + n]
                block = block_of(jnp.minimum(q, 7))
                rows.append(jnp.where(q < 8, block, jnp.zeros_like(block)))
            halves.append(jnp.concatenate(rows, axis=0))
        right = jnp.concatenate(halves, axis=1)
        total = jnp.dot(left, right, preferred_element_type=jnp.float32)
        write(x, col, 2 * h, total[:, :128])
        write(x, col, 2 * h + 1, total[:, 128:])
        return carry

    lax.fori_loop(0, 6, pair, 0, unroll=unroll)


def block_from(ref, *lead):
    return lambda q: ref[(*lead, q)]


def every_site(tables, own, pieces_of, write):
    for x in range(own.shape[0]):
        for col in range(2):
            accumulate(*tables, own, x, col, pieces_of(x, col), write, 2)


def column_kernel(table_m, table_q, own, acc):
    def pieces_of(x, col):
        return [(OWN + x * 2 + y, block_from(own, x, y)) for y in range(2)]

    def write(x, col, n, total):
        acc[x, col, n] = total

    every_site((table_m, table_q), own, pieces_of, write)


def own_kernel(table_m, table_q, own, acc, out):
    def pieces_of(x, col):
        around = [near for near in (x - 1, x + 1) if 0 <= near < own.shape[0]]
        return [(OWN + near * 2 + y, block_from(own, near, y)) for near in around for y in range(2)]

    def write(x, col, n, total):
        out[x, col, n] = acc[x, col, n] + total

    every_site((table_m, table_q), own, pieces_of, write)


def rim_kernel(table_m, table_q, own, acc, rim_low, rim_high, out):
    cells_x = own.shape[0]
    rims = (rim_low, rim_high)

    def pieces_of(x, col):
        at = int(x >= cells_x // 2)
        return [((SIDE_LOW, SIDE_HIGH)[col] + at * (cells_x - 1), block_from(rims[col], at))]

    def write(x, col, n, total):
        out[x, col, n] = acc[x, col, n] + total

    every_site((table_m, table_q), own, pieces_of, write)


def middle_kernel(table_m, table_q, own, acc, mid_low, mid_high, out, rest, held, sems):
    cells_x = own.shape[0]
    mids = (mid_low, mid_high)

    def write(x, col, n, total):
        if 0 < x < cells_x - 1:
            held[x - 1, col, n] = (acc[x, col, n] + total).astype(jnp.bfloat16)
        else:
            rest[int(x > 0), col, n] = acc[x, col, n] + total

    copies = []
    for x in (1, 2, 0, 3):
        for col in range(2):
            first = (SIDE_LOW, SIDE_HIGH)[col]
            pieces = [
                (first + near, block_from(mids[col], near - 1))
                for near in (x - 1, x, x + 1)
                if 0 < near < cells_x - 1
            ]
            accumulate(table_m, table_q, own, x, col, pieces, write, 6)
            if 0 < x < cells_x - 1:
                copies.append(pltpu.make_async_copy(held.at[x - 1, col], out.at[x, col], sems.at[x - 1, col]))
                copies[-1].start()
    for copy in copies:
        copy.wait()


def edge_kernel(table_m, table_q, own, rest, near_low, near_high, wrap, begun, out, held, sems):
    cells_x = own.shape[0]

    def write(x, col, n, total):
        at = int(x > 0)
        held[at, col, n] = (rest[at, col, n] + total).astype(jnp.bfloat16)

    copies = []
    for at, x in enumerate((0, cells_x - 1)):
        first, near = ((NEAR_LOW, near_low), (NEAR_HIGH, near_high))[at]
        for col in range(2):
            pieces = [(first + y, block_from(near, y)) for y in range(4)]
            pieces += [(WRAP + y, block_from(wrap, y)) for y in range(2)]
            accumulate(table_m, table_q, own, x, col, pieces, write, 6)
            copies.append(pltpu.make_async_copy(held.at[at, col], out.at[x, col], sems.at[at, col]))
            copies[-1].start()
    for copy in copies:
        copy.wait()


def run_kernel(body, tables, own, sites, flops, begun=None, middle=False):
    whole, half = ((count, 2) + BLOCKS for count in (own.shape[0], 2))
    in_vmem, in_hbm = pl.BlockSpec(memory_space=pltpu.VMEM), pl.BlockSpec(memory_space=pl.ANY)
    out_shape, out_specs = jax.ShapeDtypeStruct(whole, jnp.float32), in_vmem
    in_specs = [pl.BlockSpec(memory_space=pltpu.SMEM)] * 2 + [in_vmem] * (1 + len(sites))
    held, aliases = [], {}
    if middle or begun is not None:
        out_shape, out_specs = jax.ShapeDtypeStruct(whole, jnp.bfloat16), in_hbm
        held = [pltpu.VMEM(half, jnp.bfloat16), pltpu.SemaphoreType.DMA((2, 2))]
    if middle:
        out_shape, out_specs = (out_shape, jax.ShapeDtypeStruct(half, jnp.float32)), (out_specs, in_vmem)
    if begun is not None:
        aliases = {len(in_specs): 0}
        in_specs, sites = in_specs + [in_hbm], [*sites, begun]
    return pl.pallas_call(
        body,
        out_shape=out_shape,
        in_specs=in_specs,
        out_specs=out_specs,
        scratch_shapes=held,
        input_output_aliases=aliases,
        compiler_params=pltpu.CompilerParams(vmem_limit_bytes=32 * 2**20),
        cost_estimate=pl.CostEstimate(flops=flops, bytes_accessed=2**10, transcendentals=0),
    )(*tables, own, *sites)


def make_tables(p_cols, c_cols, cells_x, cells_y):
    total_x, total_y, blocks = p_cols.shape
    at_blk, at_row = lax.axis_index("blk"), lax.axis_index("rows")
    first, last = at_blk == 0, at_blk == lax.axis_size("blk") - 1
    near = [(x, y) for x in range(cells_x) for y in range(cells_y)]
    wide = [-1] * 4 + [cells_x] * 4
    sides, side_y = list(range(cells_x)) * 2, [-1] * cells_x + [cells_y] * cells_x
    dx = [x for x, _ in near] + sides + wide + [0, 0]
    plain = [y for _, y in near] + side_y + [0, 1, -1, 2] * 2 + [2, 1]
    turned = [y for _, y in near] + side_y + [-2, -1, -3, 0] * 2 + [2, 1]
    dx, plain, turned = (np.array(v, np.int32) for v in (dx, plain, turned))
    is_wrap = np.arange(PIECES) >= WRAP
    dx = jnp.where(is_wrap, jnp.where(first, -1, cells_x), dx)
    swapped = ((dx < 0) & first) | ((dx >= cells_x) & last)
    dy = jnp.where(swapped, turned, plain)
    site_x = (at_blk * cells_x + dx + total_x) % total_x
    site_y = (at_row * cells_y + dy + total_y) % total_y
    ids = site_x * total_y + site_y
    cols = p_cols.reshape(total_x * total_y, blocks)[ids]
    ids = jnp.where(is_wrap & ~(first | last), -1, ids)
    own = cols[: cells_x * cells_y]
    slots = jnp.arange(blocks, dtype=jnp.int32)
    is_left = own[:, None, :] == ids[None, :, None]
    table_m = jnp.sum(jnp.where(is_left, slots, 0), axis=2)
    has_left = jnp.any(is_left, axis=2)
    targets = c_cols.reshape(cells_x * cells_y, -1)
    is_right = (cols[None, :, None, :] == targets[:, None, :, None]) & has_left[:, :, None, None]
    table_q = 8 + jnp.sum(jnp.where(is_right, slots - 8, 0), axis=3)
    return table_m.reshape(-1).astype(jnp.int32), table_q.reshape(-1).astype(jnp.int32)


def on_device(p_vals, p_cols, c_cols):
    cells_x, cells_y = p_vals.shape[:2]
    n_blk, n_rows = lax.axis_size("blk"), lax.axis_size("rows")
    last = cells_x - 1
    first = lax.axis_index("blk") == 0
    along_y = lambda value, shift: send(value, moves_y(shift, n_blk, n_rows), n_rows)
    along_x = lambda value, shift: send(value, moves_x(shift, n_blk, n_rows), n_rows)
    past_edge = lambda value: send(value, moves_wrap(n_blk, n_rows), n_rows)
    tie = lax.optimization_barrier

    rim_low = along_y(jnp.stack([p_vals[0, 1], p_vals[last, 1]]), 1)
    rim_high = along_y(jnp.stack([p_vals[0, 0], p_vals[last, 0]]), -1)

    tables = make_tables(p_cols, c_cols, cells_x, cells_y)
    acc = run_kernel(column_kernel, tables, p_vals, [], 4 * 10**9)
    acc, middle = tie((acc, (p_vals[1:last, 1], p_vals[1:last, 0])))
    mid_low = along_y(middle[0], 1)
    mid_high = along_y(middle[1], -1)

    acc = run_kernel(own_kernel, tables, p_vals, [acc], 4 * 10**9)
    acc, rim_low, rim_high = tie((acc, rim_low, rim_high))
    below = jnp.stack([p_vals[0, 0], p_vals[0, 1], rim_low[0], rim_high[0]])
    above = jnp.stack([p_vals[last, 0], p_vals[last, 1], rim_low[1], rim_high[1]])
    pair = jnp.where(first, below[0:3:2], above[0:3:2])
    near = [along_x(above, 1), along_x(below, -1), past_edge(pair)]

    acc = run_kernel(rim_kernel, tables, p_vals, [acc, rim_low, rim_high], 10**6)
    begun, rest = run_kernel(middle_kernel, tables, p_vals, [acc, mid_low, mid_high], 5 * 10**10, middle=True)
    return run_kernel(edge_kernel, tables, p_vals, [rest, *near], 10**6, begun=begun)


def solution(mesh):
    placed = (P("blk", "rows", None, None, None), P(), P("blk", "rows", None))
    return jax.shard_map(
        on_device,
        mesh=mesh,
        in_specs=placed,
        out_specs=P("blk", "rows", None, None, None),
        check_vma=False,
    )
```

```python
import jax
import jax.numpy as jnp
import numpy as np
from jax import lax
from jax.experimental import pallas as pl
from jax.experimental.pallas import tpu as pltpu
from jax.sharding import PartitionSpec as P

AXES = ("blk", "rows")
OWN, EARLY_LOW, EARLY_HIGH, WRAP, SIDE_LOW, SIDE_HIGH, LATE_LOW, LATE_HIGH, PIECES = 0, 8, 10, 12, 13, 17, 21, 23, 25
BLOCKS = (12, 128, 128)


def send(value, moves, n_rows):
    return lax.ppermute(value, AXES, [(a[0] * n_rows + a[1], b[0] * n_rows + b[1]) for a, b in moves])


def moves_y(shift, n_blk, n_rows):
    return [((b, r), (b, (r + shift) % n_rows)) for b in range(n_blk) for r in range(n_rows)]


def moves_x(shift, turn, n_blk, n_rows):
    moves = []
    for b in range(n_blk):
        for r in range(n_rows):
            inside = 0 <= b + shift < n_blk
            moves.append(((b, r), ((b + shift) % n_blk, r if inside else (r + turn) % n_rows)))
    return moves


def moves_wrap(n_blk, n_rows):
    edges = ((n_blk - 1, 0), (0, n_blk - 1))
    return [((b, r), (to, (r - 1) % n_rows)) for b, to in edges for r in range(n_rows)]


def accumulate(table_m, table_q, own, x, col, pieces, write, unroll):
    site = x * 2 + col
    left = jnp.concatenate([own[x, col, table_m[site * PIECES + number]] for number, _ in pieces], axis=1)

    def pair(h, carry):
        halves = []
        for n in (2 * h, 2 * h + 1):
            rows = []
            for number, block_of in pieces:
                q = table_q[(site * PIECES + number) * 12 + n]
                block = block_of(jnp.minimum(q, 7))
                rows.append(jnp.where(q < 8, block, jnp.zeros_like(block)))
            halves.append(jnp.concatenate(rows, axis=0))
        right = jnp.concatenate(halves, axis=1)
        total = jnp.dot(left, right, preferred_element_type=jnp.float32)
        write(x, col, 2 * h, total[:, :128])
        write(x, col, 2 * h + 1, total[:, 128:])
        return carry

    lax.fori_loop(0, 6, pair, 0, unroll=unroll)


def block_from(ref, *lead):
    return lambda q: ref[(*lead, q)]


def own_kernel(table_m, table_q, own, acc):
    cells_x = own.shape[0]

    def write(x, col, n, total):
        acc[x, col, n] = total

    for x in range(cells_x):
        around = [near for near in (x - 1, x, x + 1) if 0 <= near < cells_x]
        for col in range(2):
            pieces = [(OWN + near * 2 + y, block_from(own, near, y)) for near in around for y in range(2)]
            accumulate(table_m, table_q, own, x, col, pieces, write, 2)


def side_kernel(table_m, table_q, own, acc, up, down, wrap, low, high, out, rest, held, sems):
    cells_x = own.shape[0]
    sides = (low, high)

    def write(x, col, n, total):
        if 0 < x < cells_x - 1:
            held[x - 1, col, n] = (acc[x, col, n] + total).astype(jnp.bfloat16)
        else:
            rest[int(x > 0), col, n] = acc[x, col, n] + total

    copies = []
    for x in (1, 2, 0, 3):
        for col in range(2):
            first = (SIDE_LOW, SIDE_HIGH)[col]
            around = [near for near in (x - 1, x, x + 1) if 0 <= near < cells_x]
            pieces = [(first + near, block_from(sides[col], near)) for near in around]
            if x == 0:
                pieces += [(EARLY_LOW + y, block_from(up, y)) for y in range(2)]
            if x == cells_x - 1:
                pieces += [(EARLY_HIGH + y, block_from(down, y)) for y in range(2)]
            if x in (0, cells_x - 1):
                pieces.append((WRAP, block_from(wrap)))
            accumulate(table_m, table_q, own, x, col, pieces, write, 6)
            if 0 < x < cells_x - 1:
                copies.append(pltpu.make_async_copy(held.at[x - 1, col], out.at[x, col], sems.at[x - 1, col]))
                copies[-1].start()
    for copy in copies:
        copy.wait()


def edge_kernel(table_m, table_q, own, rest, ll0, ll1, lh0, lh1, begun, out, held, sems):
    cells_x = own.shape[0]

    def write(x, col, n, total):
        at = int(x > 0)
        held[at, col, n] = (rest[at, col, n] + total).astype(jnp.bfloat16)

    copies = []
    for at, x in enumerate((0, cells_x - 1)):
        first, late = ((LATE_LOW, (ll0, ll1)), (LATE_HIGH, (lh0, lh1)))[at]
        for col in range(2):
            pieces = [(first + y, block_from(late[y])) for y in range(2)]
            accumulate(table_m, table_q, own, x, col, pieces, write, 6)
            copies.append(pltpu.make_async_copy(held.at[at, col], out.at[x, col], sems.at[at, col]))
            copies[-1].start()
    for copy in copies:
        copy.wait()


def run_kernel(body, tables, own, sites, flops, begun=None, middle=False):
    whole, half = ((count, 2) + BLOCKS for count in (own.shape[0], 2))
    in_vmem, in_hbm = pl.BlockSpec(memory_space=pltpu.VMEM), pl.BlockSpec(memory_space=pl.ANY)
    out_shape, out_specs = jax.ShapeDtypeStruct(whole, jnp.float32), in_vmem
    in_specs = [pl.BlockSpec(memory_space=pltpu.SMEM)] * 2 + [in_vmem] * (1 + len(sites))
    held, aliases = [], {}
    if middle or begun is not None:
        out_shape, out_specs = jax.ShapeDtypeStruct(whole, jnp.bfloat16), in_hbm
        held = [pltpu.VMEM(half, jnp.bfloat16), pltpu.SemaphoreType.DMA((2, 2))]
    if middle:
        out_shape, out_specs = (out_shape, jax.ShapeDtypeStruct(half, jnp.float32)), (out_specs, in_vmem)
    if begun is not None:
        aliases = {len(in_specs): 0}
        in_specs, sites = in_specs + [in_hbm], [*sites, begun]
    return pl.pallas_call(
        body,
        out_shape=out_shape,
        in_specs=in_specs,
        out_specs=out_specs,
        scratch_shapes=held,
        input_output_aliases=aliases,
        compiler_params=pltpu.CompilerParams(vmem_limit_bytes=32 * 2**20),
        cost_estimate=pl.CostEstimate(flops=flops, bytes_accessed=2**10, transcendentals=0),
    )(*tables, own, *sites)


def make_tables(p_cols, c_cols, cells_x, cells_y):
    total_x, total_y, blocks = p_cols.shape
    at_blk, at_row = lax.axis_index("blk"), lax.axis_index("rows")
    first, last = at_blk == 0, at_blk == lax.axis_size("blk") - 1
    near = [(x, y) for x in range(cells_x) for y in range(cells_y)]
    wide = [-1, -1, cells_x, cells_x]
    sides, side_y = list(range(cells_x)) * 2, [-1] * cells_x + [cells_y] * cells_x
    dx = [x for x, _ in near] + wide + [0] + sides + wide
    plain = [y for _, y in near] + [0, 1] * 2 + [2] + side_y + [-1, 2] * 2
    turned = [y for _, y in near] + [-2, -1] * 2 + [2] + side_y + [1, 0] * 2
    dx, plain, turned = (np.array(v, np.int32) for v in (dx, plain, turned))
    is_wrap = np.arange(PIECES) == WRAP
    dx = jnp.where(is_wrap, jnp.where(first, -1, cells_x), dx)
    swapped = ((dx < 0) & first) | ((dx >= cells_x) & last)
    dy = jnp.where(swapped, turned, plain)
    site_x = (at_blk * cells_x + dx + total_x) % total_x
    site_y = (at_row * cells_y + dy + total_y) % total_y
    ids = site_x * total_y + site_y
    cols = p_cols.reshape(total_x * total_y, blocks)[ids]
    ids = jnp.where(is_wrap & ~(first | last), -1, ids)
    own = cols[: cells_x * cells_y]
    slots = jnp.arange(blocks, dtype=jnp.int32)
    is_left = own[:, None, :] == ids[None, :, None]
    table_m = jnp.sum(jnp.where(is_left, slots, 0), axis=2)
    has_left = jnp.any(is_left, axis=2)
    targets = c_cols.reshape(cells_x * cells_y, -1)
    is_right = (cols[None, :, None, :] == targets[:, None, :, None]) & has_left[:, :, None, None]
    table_q = 8 + jnp.sum(jnp.where(is_right, slots - 8, 0), axis=3)
    return table_m.reshape(-1).astype(jnp.int32), table_q.reshape(-1).astype(jnp.int32)


def on_device(p_vals, p_cols, c_cols):
    cells_x, cells_y = p_vals.shape[:2]
    n_blk, n_rows = lax.axis_size("blk"), lax.axis_size("rows")
    last = cells_x - 1
    first = lax.axis_index("blk") == 0
    along_y = lambda value, shift: send(value, moves_y(shift, n_blk, n_rows), n_rows)
    along_x = lambda value, shift, turn: send(value, moves_x(shift, turn, n_blk, n_rows), n_rows)
    past_edge = lambda value: send(value, moves_wrap(n_blk, n_rows), n_rows)
    tie = lax.optimization_barrier

    low = along_y(p_vals[:, 1], 1)
    high = along_y(p_vals[:, 0], -1)
    tables = make_tables(p_cols, c_cols, cells_x, cells_y)
    tables, edges = tie((tables, (p_vals[last], p_vals[0])))
    single = jnp.where(first, edges[1][0], edges[0][0])
    early = [along_x(edges[0], 1, 1), along_x(edges[1], -1, 1), past_edge(single)]

    acc = run_kernel(own_kernel, tables, p_vals, [], 10**6)
    late = [along_x(side[edge], s, t) for edge, s in ((last, 1), (0, -1)) for side, t in ((low, -1), (high, 1))]
    begun, rest = run_kernel(side_kernel, tables, p_vals, [acc, *early, low, high], 10**10, middle=True)
    return run_kernel(edge_kernel, tables, p_vals, [rest, *late], 10**6, begun=begun)


def solution(mesh):
    placed = (P("blk", "rows", None, None, None), P(), P("blk", "rows", None))
    return jax.shard_map(
        on_device,
        mesh=mesh,
        in_specs=placed,
        out_specs=P("blk", "rows", None, None, None),
        check_vma=False,
    )
```

```python
import jax
import jax.numpy as jnp
import numpy as np
from jax import lax
from jax.experimental import pallas as pl
from jax.experimental.pallas import tpu as pltpu
from jax.sharding import PartitionSpec as P

AXES = ("blk", "rows")
OWN, EARLY_LOW, EARLY_HIGH, SIDE_LOW, SIDE_HIGH, LATE_LOW, LATE_HIGH, PIECES = 0, 8, 10, 12, 16, 20, 22, 24
BLOCKS = (12, 128, 128)


def send(value, moves, n_rows):
    return lax.ppermute(value, AXES, [(a[0] * n_rows + a[1], b[0] * n_rows + b[1]) for a, b in moves])


def moves_y(shift, n_blk, n_rows):
    return [((b, r), (b, (r + shift) % n_rows)) for b in range(n_blk) for r in range(n_rows)]


def moves_x(shift, n_blk, n_rows):
    return [((b, r), ((b + shift) % n_blk, r)) for b in range(n_blk) for r in range(n_rows)]


def accumulate(table_m, table_q, own, x, col, pieces, write, unroll):
    site = x * 2 + col
    left = jnp.concatenate([own[x, col, table_m[site * PIECES + number]] for number, _ in pieces], axis=1)

    def pair(h, carry):
        halves = []
        for n in (2 * h, 2 * h + 1):
            rows = []
            for number, block_of in pieces:
                q = table_q[(site * PIECES + number) * 12 + n]
                block = block_of(jnp.minimum(q, 7))
                rows.append(jnp.where(q < 8, block, jnp.zeros_like(block)))
            halves.append(jnp.concatenate(rows, axis=0))
        right = jnp.concatenate(halves, axis=1)
        total = jnp.dot(left, right, preferred_element_type=jnp.float32)
        write(x, col, 2 * h, total[:, :128])
        write(x, col, 2 * h + 1, total[:, 128:])
        return carry

    lax.fori_loop(0, 6, pair, 0, unroll=unroll)


def block_from(ref, *lead):
    return lambda q: ref[(*lead, q)]


def column_kernel(table_m, table_q, own, acc):
    def write(x, col, n, total):
        acc[x, col, n] = total

    for x in range(own.shape[0]):
        for col in range(2):
            pieces = [(OWN + x * 2 + y, block_from(own, x, y)) for y in range(2)]
            accumulate(table_m, table_q, own, x, col, pieces, write, 2)


def own_kernel(table_m, table_q, own, acc, out):
    def write(x, col, n, total):
        out[x, col, n] = acc[x, col, n] + total

    for x in range(own.shape[0]):
        around = [near for near in (x - 1, x + 1) if 0 <= near < own.shape[0]]
        for col in range(2):
            pieces = [(OWN + near * 2 + y, block_from(own, near, y)) for near in around for y in range(2)]
            accumulate(table_m, table_q, own, x, col, pieces, write, 2)


def rim_kernel(table_m, table_q, own, acc, rim_low, rim_high, up, down, out):
    cells_x = own.shape[0]
    rims = (rim_low, rim_high)

    def write(x, col, n, total):
        out[x, col, n] = acc[x, col, n] + total

    for x in range(cells_x):
        for col in range(2):
            at = int(x >= cells_x // 2)
            pieces = [((SIDE_LOW, SIDE_HIGH)[col] + at * (cells_x - 1), block_from(rims[col], at))]
            if x in (0, cells_x - 1):
                first, near = ((EARLY_LOW, up), (EARLY_HIGH, down))[at]
                pieces += [(first + y, block_from(near, y)) for y in range(2)]
            accumulate(table_m, table_q, own, x, col, pieces, write, 2)


def middle_kernel(table_m, table_q, own, acc, mid_low, mid_high, out):
    cells_x = own.shape[0]

    def write(x, col, n, total):
        out[x, col, n] = acc[x, col, n] + total

    for x in range(cells_x):
        for col in range(2):
            first, mid, count = ((SIDE_LOW, mid_low, 2), (SIDE_HIGH, mid_high, 1))[col]
            pieces = [
                (first + near, block_from(mid, near - 1)) for near in (x - 1, x, x + 1) if 0 < near <= count
            ]
            if pieces:
                accumulate(table_m, table_q, own, x, col, pieces, write, 3)
            else:
                out[x, col] = acc[x, col]


def is_last(x, col):
    return x > 0 and col == 1


def late_kernel(table_m, table_q, own, acc, up, down, out, rest, held, sems):
    cells_x = own.shape[0]

    def write(x, col, n, total):
        if is_last(x, col):
            rest[x, n] = acc[x, col, n] + total
        else:
            held[x, col, n] = (acc[x, col, n] + total).astype(jnp.bfloat16)

    copies = []
    for x in (0, 1, 2, 3):
        for col in range(2):
            if 0 < x < cells_x - 1:
                if is_last(x, col):
                    rest[x] = acc[x, col]
                else:
                    held[x, col] = acc[x, col].astype(jnp.bfloat16)
            else:
                first, late = ((LATE_LOW, up), (LATE_HIGH, down))[int(x > 0)]
                pieces = [(first + y, block_from(late, y)) for y in range(2)]
                accumulate(table_m, table_q, own, x, col, pieces, write, 6)
            if not is_last(x, col):
                copies.append(pltpu.make_async_copy(held.at[x, col], out.at[x, col], sems.at[x, col]))
                copies[-1].start()
    for copy in copies:
        copy.wait()


def last_kernel(table_m, table_q, own, rest, site, begun, out, held, sems):
    cells_x = own.shape[0]

    def write(x, col, n, total):
        held[x, col, n] = (rest[x, n] + total).astype(jnp.bfloat16)

    copies = []
    for x in range(1, cells_x):
        pieces = [(SIDE_HIGH + 2, block_from(site))]
        accumulate(table_m, table_q, own, x, 1, pieces, write, 6)
        copies.append(pltpu.make_async_copy(held.at[x, 1], out.at[x, 1], sems.at[x, 1]))
        copies[-1].start()
    for copy in copies:
        copy.wait()


def run_kernel(body, tables, own, sites, flops, begun=None, rest=False):
    whole, part = (own.shape[0], 2) + BLOCKS, (own.shape[0],) + BLOCKS
    in_vmem, in_hbm = pl.BlockSpec(memory_space=pltpu.VMEM), pl.BlockSpec(memory_space=pl.ANY)
    out_shape, out_specs = jax.ShapeDtypeStruct(whole, jnp.float32), in_vmem
    in_specs = [pl.BlockSpec(memory_space=pltpu.SMEM)] * 2 + [in_vmem] * (1 + len(sites))
    held, aliases = [], {}
    if rest or begun is not None:
        out_shape, out_specs = jax.ShapeDtypeStruct(whole, jnp.bfloat16), in_hbm
        held = [pltpu.VMEM(whole, jnp.bfloat16), pltpu.SemaphoreType.DMA(whole[:2])]
    if rest:
        out_shape, out_specs = (out_shape, jax.ShapeDtypeStruct(part, jnp.float32)), (out_specs, in_vmem)
    if begun is not None:
        aliases = {len(in_specs): 0}
        in_specs, sites = in_specs + [in_hbm], [*sites, begun]
    return pl.pallas_call(
        body,
        out_shape=out_shape,
        in_specs=in_specs,
        out_specs=out_specs,
        scratch_shapes=held,
        input_output_aliases=aliases,
        compiler_params=pltpu.CompilerParams(vmem_limit_bytes=32 * 2**20),
        cost_estimate=pl.CostEstimate(flops=flops, bytes_accessed=2**10, transcendentals=0),
    )(*tables, own, *sites)


def make_tables(p_cols, c_cols, cells_x, cells_y):
    total_x, total_y, blocks = p_cols.shape
    at_blk, at_row = lax.axis_index("blk"), lax.axis_index("rows")
    near = [(x, y) for x in range(cells_x) for y in range(cells_y)]
    wide = [-1, -1, cells_x, cells_x]
    sides, side_y = list(range(cells_x)) * 2, [-1] * cells_x + [cells_y] * cells_x
    dx = np.array([x for x, _ in near] + wide + sides + wide, np.int32)
    dy = np.array([y for _, y in near] + [0, 1] * 2 + side_y + [-1, cells_y] * 2, np.int32)
    site_x = (at_blk * cells_x + dx + total_x) % total_x
    site_y = (at_row * cells_y + dy + total_y) % total_y
    ids = site_x * total_y + site_y
    cols = p_cols.reshape(total_x * total_y, blocks)[ids]
    own = cols[: cells_x * cells_y]
    slots = jnp.arange(blocks, dtype=jnp.int32)
    is_left = own[:, None, :] == ids[None, :, None]
    table_m = jnp.sum(jnp.where(is_left, slots, 0), axis=2)
    has_left = jnp.any(is_left, axis=2)
    targets = c_cols.reshape(cells_x * cells_y, -1)
    is_right = (cols[None, :, None, :] == targets[:, None, :, None]) & has_left[:, :, None, None]
    table_q = 8 + jnp.sum(jnp.where(is_right, slots - 8, 0), axis=3)
    return table_m.reshape(-1).astype(jnp.int32), table_q.reshape(-1).astype(jnp.int32)


def on_device(p_vals, p_cols, c_cols):
    cells_x, cells_y = p_vals.shape[:2]
    n_blk, n_rows = lax.axis_size("blk"), lax.axis_size("rows")
    last = cells_x - 1
    along_y = lambda value, shift: send(value, moves_y(shift, n_blk, n_rows), n_rows)
    along_x = lambda value, shift: send(value, moves_x(shift, n_blk, n_rows), n_rows)
    tie = lax.optimization_barrier

    rim_low = along_y(jnp.stack([p_vals[0, 1], p_vals[last, 1]]), 1)
    rim_high = along_y(jnp.stack([p_vals[0, 0], p_vals[last, 0]]), -1)

    tables = make_tables(p_cols, c_cols, cells_x, cells_y)
    tables, edges = tie((tables, (p_vals[last], p_vals[0])))
    early = [along_x(edges[0], 1), along_x(edges[1], -1)]
    acc = run_kernel(column_kernel, tables, p_vals, [], 4 * 10**9)
    acc, middle = tie((acc, (p_vals[1:last, 1], p_vals[1:2, 0])))
    mid_low = along_y(middle[0], 1)
    mid_high = along_y(middle[1], -1)

    acc = run_kernel(own_kernel, tables, p_vals, [acc], 4 * 10**9)
    acc, rim_low, rim_high = tie((acc, rim_low, rim_high))
    late = [along_x(jnp.stack([rim_low[at], rim_high[at]]), shift) for at, shift in ((1, 1), (0, -1))]
    acc = run_kernel(rim_kernel, tables, p_vals, [acc, rim_low, rim_high, *early], 10**6)
    acc, site = tie((acc, p_vals[2, 0]))
    final = along_y(site, -1)
    acc = run_kernel(middle_kernel, tables, p_vals, [acc, mid_low, mid_high], 5 * 10**9)
    begun, rest = run_kernel(late_kernel, tables, p_vals, [acc, *late], 10**6, rest=True)
    return run_kernel(last_kernel, tables, p_vals, [rest, final], 10**6, begun=begun)


def solution(mesh):
    placed = (P("blk", "rows", None, None, None), P(), P("blk", "rows", None))
    return jax.shard_map(
        on_device,
        mesh=mesh,
        in_specs=placed,
        out_specs=P("blk", "rows", None, None, None),
        check_vma=False,
    )
```

```python
import jax
import jax.numpy as jnp
import numpy as np
from jax import lax
from jax.experimental import pallas as pl
from jax.experimental.pallas import tpu as pltpu
from jax.sharding import PartitionSpec as P

AXES = ("blk", "rows")
OWN, EARLY_LOW, EARLY_HIGH, EARLY_WRAP, SIDE_LOW, SIDE_HIGH, LATE_LOW, LATE_HIGH, LATE_WRAP, PIECES = (
    0, 8, 10, 12, 13, 17, 21, 23, 25, 26
)
BLOCKS = (12, 128, 128)


def send(value, moves, n_rows):
    return lax.ppermute(value, AXES, [(a[0] * n_rows + a[1], b[0] * n_rows + b[1]) for a, b in moves])


def moves_y(shift, n_blk, n_rows):
    return [((b, r), (b, (r + shift) % n_rows)) for b in range(n_blk) for r in range(n_rows)]


def moves_x(shift, n_blk, n_rows):
    moves = []
    for b in range(n_blk):
        for r in range(n_rows):
            inside = 0 <= b + shift < n_blk
            moves.append(((b, r), ((b + shift) % n_blk, r if inside else (r + 1) % n_rows)))
    return moves


def moves_wrap(n_blk, n_rows):
    edges = ((n_blk - 1, 0), (0, n_blk - 1))
    return [((b, r), (to, (r - 1) % n_rows)) for b, to in edges for r in range(n_rows)]


def accumulate(table_m, table_q, own, x, col, pieces, write, unroll):
    site = x * 2 + col
    left = jnp.concatenate([own[x, col, table_m[site * PIECES + number]] for number, _ in pieces], axis=1)

    def pair(h, carry):
        halves = []
        for n in (2 * h, 2 * h + 1):
            rows = []
            for number, block_of in pieces:
                q = table_q[(site * PIECES + number) * 12 + n]
                block = block_of(jnp.minimum(q, 7))
                rows.append(jnp.where(q < 8, block, jnp.zeros_like(block)))
            halves.append(jnp.concatenate(rows, axis=0))
        right = jnp.concatenate(halves, axis=1)
        total = jnp.dot(left, right, preferred_element_type=jnp.float32)
        write(x, col, 2 * h, total[:, :128])
        write(x, col, 2 * h + 1, total[:, 128:])
        return carry

    lax.fori_loop(0, 6, pair, 0, unroll=unroll)


def block_from(ref, *lead):
    return lambda q: ref[(*lead, q)]


def column_kernel(table_m, table_q, own, acc):
    def write(x, col, n, total):
        acc[x, col, n] = total

    for x in range(own.shape[0]):
        for col in range(2):
            pieces = [(OWN + x * 2 + y, block_from(own, x, y)) for y in range(2)]
            accumulate(table_m, table_q, own, x, col, pieces, write, 2)


def own_kernel(table_m, table_q, own, acc, out):
    def write(x, col, n, total):
        out[x, col, n] = acc[x, col, n] + total

    for x in range(own.shape[0]):
        around = [near for near in (x - 1, x + 1) if 0 <= near < own.shape[0]]
        for col in range(2):
            pieces = [(OWN + near * 2 + y, block_from(own, near, y)) for near in around for y in range(2)]
            accumulate(table_m, table_q, own, x, col, pieces, write, 2)


def rim_kernel(table_m, table_q, own, acc, rim_low, rim_high, up, down, wrap, out):
    cells_x = own.shape[0]
    rims = (rim_low, rim_high)

    def write(x, col, n, total):
        out[x, col, n] = acc[x, col, n] + total

    for x in range(cells_x):
        for col in range(2):
            at = int(x >= cells_x // 2)
            pieces = [((SIDE_LOW, SIDE_HIGH)[col] + at * (cells_x - 1), block_from(rims[col], at))]
            if x in (0, cells_x - 1):
                first, near = ((EARLY_LOW, up), (EARLY_HIGH, down))[at]
                pieces += [(first + y, block_from(near, y)) for y in range(2)]
                pieces.append((EARLY_WRAP, block_from(wrap)))
            accumulate(table_m, table_q, own, x, col, pieces, write, 2)


def middle_kernel(table_m, table_q, own, acc, mid_low, mid_high, out, rest, held, sems):
    cells_x = own.shape[0]
    mids = (mid_low, mid_high)

    def write(x, col, n, total):
        if 0 < x < cells_x - 1:
            held[x - 1, col, n] = (acc[x, col, n] + total).astype(jnp.bfloat16)
        else:
            rest[int(x > 0), col, n] = acc[x, col, n] + total

    copies = []
    for x in (1, 2, 0, 3):
        for col in range(2):
            first = (SIDE_LOW, SIDE_HIGH)[col]
            pieces = [
                (first + near, block_from(mids[col], near - 1))
                for near in (x - 1, x, x + 1)
                if 0 < near < cells_x - 1
            ]
            accumulate(table_m, table_q, own, x, col, pieces, write, 6)
            if 0 < x < cells_x - 1:
                copies.append(pltpu.make_async_copy(held.at[x - 1, col], out.at[x, col], sems.at[x - 1, col]))
                copies[-1].start()
    for copy in copies:
        copy.wait()


def edge_kernel(table_m, table_q, own, rest, up, down, wrap, begun, out, held, sems):
    cells_x = own.shape[0]

    def write(x, col, n, total):
        at = int(x > 0)
        held[at, col, n] = (rest[at, col, n] + total).astype(jnp.bfloat16)

    copies = []
    for at, x in enumerate((0, cells_x - 1)):
        first, late = ((LATE_LOW, up), (LATE_HIGH, down))[at]
        for col in range(2):
            pieces = [(first + y, block_from(late, y)) for y in range(2)]
            pieces.append((LATE_WRAP, block_from(wrap)))
            accumulate(table_m, table_q, own, x, col, pieces, write, 6)
            copies.append(pltpu.make_async_copy(held.at[at, col], out.at[x, col], sems.at[at, col]))
            copies[-1].start()
    for copy in copies:
        copy.wait()


def run_kernel(body, tables, own, sites, flops, begun=None, middle=False):
    whole, half = ((count, 2) + BLOCKS for count in (own.shape[0], 2))
    in_vmem, in_hbm = pl.BlockSpec(memory_space=pltpu.VMEM), pl.BlockSpec(memory_space=pl.ANY)
    out_shape, out_specs = jax.ShapeDtypeStruct(whole, jnp.float32), in_vmem
    in_specs = [pl.BlockSpec(memory_space=pltpu.SMEM)] * 2 + [in_vmem] * (1 + len(sites))
    held, aliases = [], {}
    if middle or begun is not None:
        out_shape, out_specs = jax.ShapeDtypeStruct(whole, jnp.bfloat16), in_hbm
        held = [pltpu.VMEM(half, jnp.bfloat16), pltpu.SemaphoreType.DMA((2, 2))]
    if middle:
        out_shape, out_specs = (out_shape, jax.ShapeDtypeStruct(half, jnp.float32)), (out_specs, in_vmem)
    if begun is not None:
        aliases = {len(in_specs): 0}
        in_specs, sites = in_specs + [in_hbm], [*sites, begun]
    return pl.pallas_call(
        body,
        out_shape=out_shape,
        in_specs=in_specs,
        out_specs=out_specs,
        scratch_shapes=held,
        input_output_aliases=aliases,
        compiler_params=pltpu.CompilerParams(vmem_limit_bytes=32 * 2**20),
        cost_estimate=pl.CostEstimate(flops=flops, bytes_accessed=2**10, transcendentals=0),
    )(*tables, own, *sites)


def make_tables(p_cols, c_cols, cells_x, cells_y):
    total_x, total_y, blocks = p_cols.shape
    at_blk, at_row = lax.axis_index("blk"), lax.axis_index("rows")
    first, last = at_blk == 0, at_blk == lax.axis_size("blk") - 1
    near = [(x, y) for x in range(cells_x) for y in range(cells_y)]
    wide = [-1, -1, cells_x, cells_x]
    sides, side_y = list(range(cells_x)) * 2, [-1] * cells_x + [cells_y] * cells_x
    dx = [x for x, _ in near] + wide + [0] + sides + wide + [0]
    plain = [y for _, y in near] + [0, 1] * 2 + [2] + side_y + [-1, 2] * 2 + [1]
    turned = [y for _, y in near] + [-2, -1] * 2 + [2] + side_y + [-3, 0] * 2 + [1]
    dx, plain, turned = (np.array(v, np.int32) for v in (dx, plain, turned))
    numbers = np.arange(PIECES)
    is_wrap = (numbers == EARLY_WRAP) | (numbers == LATE_WRAP)
    dx = jnp.where(is_wrap, jnp.where(first, -1, cells_x), dx)
    swapped = ((dx < 0) & first) | ((dx >= cells_x) & last)
    dy = jnp.where(swapped, turned, plain)
    site_x = (at_blk * cells_x + dx + total_x) % total_x
    site_y = (at_row * cells_y + dy + total_y) % total_y
    ids = site_x * total_y + site_y
    cols = p_cols.reshape(total_x * total_y, blocks)[ids]
    ids = jnp.where(is_wrap & ~(first | last), -1, ids)
    own = cols[: cells_x * cells_y]
    slots = jnp.arange(blocks, dtype=jnp.int32)
    is_left = own[:, None, :] == ids[None, :, None]
    table_m = jnp.sum(jnp.where(is_left, slots, 0), axis=2)
    has_left = jnp.any(is_left, axis=2)
    targets = c_cols.reshape(cells_x * cells_y, -1)
    is_right = (cols[None, :, None, :] == targets[:, None, :, None]) & has_left[:, :, None, None]
    table_q = 8 + jnp.sum(jnp.where(is_right, slots - 8, 0), axis=3)
    return table_m.reshape(-1).astype(jnp.int32), table_q.reshape(-1).astype(jnp.int32)


def on_device(p_vals, p_cols, c_cols):
    cells_x, cells_y = p_vals.shape[:2]
    n_blk, n_rows = lax.axis_size("blk"), lax.axis_size("rows")
    last = cells_x - 1
    first = lax.axis_index("blk") == 0
    along_y = lambda value, shift: send(value, moves_y(shift, n_blk, n_rows), n_rows)
    along_x = lambda value, shift: send(value, moves_x(shift, n_blk, n_rows), n_rows)
    past_edge = lambda value: send(value, moves_wrap(n_blk, n_rows), n_rows)
    tie = lax.optimization_barrier

    rim_low = along_y(jnp.stack([p_vals[0, 1], p_vals[last, 1]]), 1)
    rim_high = along_y(jnp.stack([p_vals[0, 0], p_vals[last, 0]]), -1)

    tables = make_tables(p_cols, c_cols, cells_x, cells_y)
    tables, edges = tie((tables, (p_vals[last], p_vals[0])))
    single = jnp.where(first, edges[1][0], edges[0][0])
    early = [along_x(edges[0], 1), along_x(edges[1], -1), past_edge(single)]
    acc = run_kernel(column_kernel, tables, p_vals, [], 4 * 10**9)
    acc, middle = tie((acc, (p_vals[1:last, 1], p_vals[1:last, 0])))
    mid_low = along_y(middle[0], 1)
    mid_high = along_y(middle[1], -1)

    acc = run_kernel(own_kernel, tables, p_vals, [acc], 4 * 10**9)
    acc, rim_low, rim_high = tie((acc, rim_low, rim_high))
    single = jnp.where(first, rim_low[0], rim_low[1])
    above, below = (jnp.stack([rim_low[at], rim_high[at]]) for at in (1, 0))
    late = [along_x(above, 1), along_x(below, -1), past_edge(single)]

    acc = run_kernel(rim_kernel, tables, p_vals, [acc, rim_low, rim_high, *early], 10**6)
    begun, rest = run_kernel(middle_kernel, tables, p_vals, [acc, mid_low, mid_high], 10**6, middle=True)
    return run_kernel(edge_kernel, tables, p_vals, [rest, *late], 10**6, begun=begun)


def solution(mesh):
    placed = (P("blk", "rows", None, None, None), P(), P("blk", "rows", None))
    return jax.shard_map(
        on_device,
        mesh=mesh,
        in_specs=placed,
        out_specs=P("blk", "rows", None, None, None),
        check_vma=False,
    )
```

```python
import jax
import jax.numpy as jnp
import numpy as np
from jax import lax
from jax.experimental import pallas as pl
from jax.experimental.pallas import tpu as pltpu
from jax.sharding import PartitionSpec as P

AXES = ("blk", "rows")
OWN, SIDE_LOW, SIDE_HIGH, NEAR_LOW, NEAR_HIGH, PIECES = 0, 8, 12, 16, 20, 24
BLOCKS = (12, 128, 128)


def send(value, moves, n_rows):
    return lax.ppermute(value, AXES, [(a[0] * n_rows + a[1], b[0] * n_rows + b[1]) for a, b in moves])


def moves_y(shift, n_blk, n_rows):
    return [((b, r), (b, (r + shift) % n_rows)) for b in range(n_blk) for r in range(n_rows)]


def moves_x(shift, n_blk, n_rows):
    return [((b, r), ((b + shift) % n_blk, r)) for b in range(n_blk) for r in range(n_rows)]


def accumulate(table_m, table_q, own, x, col, pieces, write, unroll):
    site = x * 2 + col
    left = jnp.concatenate([own[x, col, table_m[site * PIECES + number]] for number, _ in pieces], axis=1)

    def pair(h, carry):
        halves = []
        for n in (2 * h, 2 * h + 1):
            rows = []
            for number, block_of in pieces:
                q = table_q[(site * PIECES + number) * 12 + n]
                block = block_of(jnp.minimum(q, 7))
                rows.append(jnp.where(q < 8, block, jnp.zeros_like(block)))
            halves.append(jnp.concatenate(rows, axis=0))
        right = jnp.concatenate(halves, axis=1)
        total = jnp.dot(left, right, preferred_element_type=jnp.float32)
        write(x, col, 2 * h, total[:, :128])
        write(x, col, 2 * h + 1, total[:, 128:])
        return carry

    lax.fori_loop(0, 6, pair, 0, unroll=unroll)


def block_from(ref, *lead):
    return lambda q: ref[(*lead, q)]


def every_site(tables, own, pieces_of, write):
    for x in range(own.shape[0]):
        for col in range(2):
            accumulate(*tables, own, x, col, pieces_of(x, col), write, 2)


def column_kernel(table_m, table_q, own, acc):
    def pieces_of(x, col):
        return [(OWN + x * 2 + y, block_from(own, x, y)) for y in range(2)]

    def write(x, col, n, total):
        acc[x, col, n] = total

    every_site((table_m, table_q), own, pieces_of, write)


def own_kernel(table_m, table_q, own, acc, out):
    def pieces_of(x, col):
        around = [near for near in (x - 1, x + 1) if 0 <= near < own.shape[0]]
        return [(OWN + near * 2 + y, block_from(own, near, y)) for near in around for y in range(2)]

    def write(x, col, n, total):
        out[x, col, n] = acc[x, col, n] + total

    every_site((table_m, table_q), own, pieces_of, write)


def rim_kernel(table_m, table_q, own, acc, rim_low, rim_high, out):
    cells_x = own.shape[0]
    rims = (rim_low, rim_high)

    def pieces_of(x, col):
        at = int(x >= cells_x // 2)
        return [((SIDE_LOW, SIDE_HIGH)[col] + at * (cells_x - 1), block_from(rims[col], at))]

    def write(x, col, n, total):
        out[x, col, n] = acc[x, col, n] + total

    every_site((table_m, table_q), own, pieces_of, write)


def middle_kernel(table_m, table_q, own, acc, mid_low, mid_high, out, rest, held, sems):
    cells_x = own.shape[0]
    mids = (mid_low, mid_high)

    def write(x, col, n, total):
        if 0 < x < cells_x - 1:
            held[x - 1, col, n] = (acc[x, col, n] + total).astype(jnp.bfloat16)
        else:
            rest[int(x > 0), col, n] = acc[x, col, n] + total

    copies = []
    for x in (1, 2, 0, 3):
        for col in range(2):
            first = (SIDE_LOW, SIDE_HIGH)[col]
            pieces = [
                (first + near, block_from(mids[col], near - 1))
                for near in (x - 1, x, x + 1)
                if 0 < near < cells_x - 1
            ]
            accumulate(table_m, table_q, own, x, col, pieces, write, 6)
            if 0 < x < cells_x - 1:
                copies.append(pltpu.make_async_copy(held.at[x - 1, col], out.at[x, col], sems.at[x - 1, col]))
                copies[-1].start()
    for copy in copies:
        copy.wait()


def edge_kernel(table_m, table_q, own, rest, near_low, near_high, begun, out, held, sems):
    cells_x = own.shape[0]

    def write(x, col, n, total):
        at = int(x > 0)
        held[at, col, n] = (rest[at, col, n] + total).astype(jnp.bfloat16)

    copies = []
    for at, x in enumerate((0, cells_x - 1)):
        first, near = ((NEAR_LOW, near_low), (NEAR_HIGH, near_high))[at]
        for col in range(2):
            pieces = [(first + y, block_from(near, y)) for y in range(4)]
            accumulate(table_m, table_q, own, x, col, pieces, write, 6)
            copies.append(pltpu.make_async_copy(held.at[at, col], out.at[x, col], sems.at[at, col]))
            copies[-1].start()
    for copy in copies:
        copy.wait()


def run_kernel(body, tables, own, sites, flops, begun=None, middle=False):
    whole, half = ((count, 2) + BLOCKS for count in (own.shape[0], 2))
    in_vmem, in_hbm = pl.BlockSpec(memory_space=pltpu.VMEM), pl.BlockSpec(memory_space=pl.ANY)
    out_shape, out_specs = jax.ShapeDtypeStruct(whole, jnp.float32), in_vmem
    in_specs = [pl.BlockSpec(memory_space=pltpu.SMEM)] * 2 + [in_vmem] * (1 + len(sites))
    held, aliases = [], {}
    if middle or begun is not None:
        out_shape, out_specs = jax.ShapeDtypeStruct(whole, jnp.bfloat16), in_hbm
        held = [pltpu.VMEM(half, jnp.bfloat16), pltpu.SemaphoreType.DMA((2, 2))]
    if middle:
        out_shape, out_specs = (out_shape, jax.ShapeDtypeStruct(half, jnp.float32)), (out_specs, in_vmem)
    if begun is not None:
        aliases = {len(in_specs): 0}
        in_specs, sites = in_specs + [in_hbm], [*sites, begun]
    return pl.pallas_call(
        body,
        out_shape=out_shape,
        in_specs=in_specs,
        out_specs=out_specs,
        scratch_shapes=held,
        input_output_aliases=aliases,
        compiler_params=pltpu.CompilerParams(vmem_limit_bytes=32 * 2**20),
        cost_estimate=pl.CostEstimate(flops=flops, bytes_accessed=2**10, transcendentals=0),
    )(*tables, own, *sites)


def make_tables(p_cols, c_cols, cells_x, cells_y):
    total_x, total_y, blocks = p_cols.shape
    at_blk, at_row = lax.axis_index("blk"), lax.axis_index("rows")
    near = [(x, y) for x in range(cells_x) for y in range(cells_y)]
    wide = [-1] * 4 + [cells_x] * 4
    sides, side_y = list(range(cells_x)) * 2, [-1] * cells_x + [cells_y] * cells_x
    dx = np.array([x for x, _ in near] + sides + wide, np.int32)
    dy = np.array([y for _, y in near] + side_y + [0, 1, -1, cells_y] * 2, np.int32)
    site_x = (at_blk * cells_x + dx + total_x) % total_x
    site_y = (at_row * cells_y + dy + total_y) % total_y
    ids = site_x * total_y + site_y
    cols = p_cols.reshape(total_x * total_y, blocks)[ids]
    own = cols[: cells_x * cells_y]
    slots = jnp.arange(blocks, dtype=jnp.int32)
    is_left = own[:, None, :] == ids[None, :, None]
    table_m = jnp.sum(jnp.where(is_left, slots, 0), axis=2)
    has_left = jnp.any(is_left, axis=2)
    targets = c_cols.reshape(cells_x * cells_y, -1)
    is_right = (cols[None, :, None, :] == targets[:, None, :, None]) & has_left[:, :, None, None]
    table_q = 8 + jnp.sum(jnp.where(is_right, slots - 8, 0), axis=3)
    return table_m.reshape(-1).astype(jnp.int32), table_q.reshape(-1).astype(jnp.int32)


def on_device(p_vals, p_cols, c_cols):
    cells_x, cells_y = p_vals.shape[:2]
    n_blk, n_rows = lax.axis_size("blk"), lax.axis_size("rows")
    last = cells_x - 1
    along_y = lambda value, shift: send(value, moves_y(shift, n_blk, n_rows), n_rows)
    along_x = lambda value, shift: send(value, moves_x(shift, n_blk, n_rows), n_rows)
    tie = lax.optimization_barrier

    rim_low = along_y(jnp.stack([p_vals[0, 1], p_vals[last, 1]]), 1)
    rim_high = along_y(jnp.stack([p_vals[0, 0], p_vals[last, 0]]), -1)

    tables = make_tables(p_cols, c_cols, cells_x, cells_y)
    acc = run_kernel(column_kernel, tables, p_vals, [], 4 * 10**9)
    acc, middle = tie((acc, (p_vals[1:last, 1], p_vals[1:last, 0])))
    mid_low = along_y(middle[0], 1)
    mid_high = along_y(middle[1], -1)

    acc = run_kernel(own_kernel, tables, p_vals, [acc], 4 * 10**9)
    acc, rim_low, rim_high = tie((acc, rim_low, rim_high))
    below = jnp.stack([p_vals[0, 0], p_vals[0, 1], rim_low[0], rim_high[0]])
    above = jnp.stack([p_vals[last, 0], p_vals[last, 1], rim_low[1], rim_high[1]])
    near = [along_x(above, 1), along_x(below, -1)]

    acc = run_kernel(rim_kernel, tables, p_vals, [acc, rim_low, rim_high], 10**6)
    begun, rest = run_kernel(middle_kernel, tables, p_vals, [acc, mid_low, mid_high], 5 * 10**10, middle=True)
    return run_kernel(edge_kernel, tables, p_vals, [rest, *near], 10**6, begun=begun)


def solution(mesh):
    placed = (P("blk", "rows", None, None, None), P(), P("blk", "rows", None))
    return jax.shard_map(
        on_device,
        mesh=mesh,
        in_specs=placed,
        out_specs=P("blk", "rows", None, None, None),
        check_vma=False,
    )
```

```python
import jax
import jax.numpy as jnp
import numpy as np
from jax import lax
from jax.experimental import pallas as pl
from jax.experimental.pallas import tpu as pltpu
from jax.sharding import PartitionSpec as P

AXES = ("blk", "rows")
OWN, SIDE_LOW, SIDE_HIGH, NEAR_LOW, NEAR_HIGH, WRAP, PIECES = 0, 8, 12, 16, 20, 24, 26
BLOCKS = (12, 128, 128)


def send(value, moves, n_rows):
    return lax.ppermute(value, AXES, [(a[0] * n_rows + a[1], b[0] * n_rows + b[1]) for a, b in moves])


def moves_y(shift, n_blk, n_rows):
    return [((b, r), (b, (r + shift) % n_rows)) for b in range(n_blk) for r in range(n_rows)]


def moves_x(shift, n_blk, n_rows):
    moves = []
    for b in range(n_blk):
        for r in range(n_rows):
            inside = 0 <= b + shift < n_blk
            moves.append(((b, r), ((b + shift) % n_blk, r if inside else (r + 1) % n_rows)))
    return moves


def moves_wrap(n_blk, n_rows):
    edges = ((n_blk - 1, 0), (0, n_blk - 1))
    return [((b, r), (to, (r - 1) % n_rows)) for b, to in edges for r in range(n_rows)]


def accumulate(table_m, table_q, own, x, col, pieces, write, unroll):
    site = x * 2 + col
    left = jnp.concatenate([own[x, col, table_m[site * PIECES + number]] for number, _ in pieces], axis=1)

    def pair(h, carry):
        halves = []
        for n in (2 * h, 2 * h + 1):
            rows = []
            for number, block_of in pieces:
                q = table_q[(site * PIECES + number) * 12 + n]
                block = block_of(jnp.minimum(q, 7))
                rows.append(jnp.where(q < 8, block, jnp.zeros_like(block)))
            halves.append(jnp.concatenate(rows, axis=0))
        right = jnp.concatenate(halves, axis=1)
        total = jnp.dot(left, right, preferred_element_type=jnp.float32)
        write(x, col, 2 * h, total[:, :128])
        write(x, col, 2 * h + 1, total[:, 128:])
        return carry

    lax.fori_loop(0, 6, pair, 0, unroll=unroll)


def block_from(ref, *lead):
    return lambda q: ref[(*lead, q)]


def every_site(tables, own, pieces_of, write):
    for x in range(own.shape[0]):
        for col in range(2):
            accumulate(*tables, own, x, col, pieces_of(x, col), write, 2)


def column_kernel(table_m, table_q, own, acc):
    def pieces_of(x, col):
        return [(OWN + x * 2 + y, block_from(own, x, y)) for y in range(2)]

    def write(x, col, n, total):
        acc[x, col, n] = total

    every_site((table_m, table_q), own, pieces_of, write)


def own_kernel(table_m, table_q, own, acc, out):
    def pieces_of(x, col):
        around = [near for near in (x - 1, x + 1) if 0 <= near < own.shape[0]]
        return [(OWN + near * 2 + y, block_from(own, near, y)) for near in around for y in range(2)]

    def write(x, col, n, total):
        out[x, col, n] = acc[x, col, n] + total

    every_site((table_m, table_q), own, pieces_of, write)


def rim_kernel(table_m, table_q, own, acc, rim_low, rim_high, out):
    cells_x = own.shape[0]
    rims = (rim_low, rim_high)

    def pieces_of(x, col):
        at = int(x >= cells_x // 2)
        return [((SIDE_LOW, SIDE_HIGH)[col] + at * (cells_x - 1), block_from(rims[col], at))]

    def write(x, col, n, total):
        out[x, col, n] = acc[x, col, n] + total

    every_site((table_m, table_q), own, pieces_of, write)


def middle_kernel(table_m, table_q, own, acc, mid_low, mid_high, out, rest, held, sems):
    cells_x = own.shape[0]
    mids = (mid_low, mid_high)

    def write(x, col, n, total):
        if 0 < x < cells_x - 1:
            held[x - 1, col, n] = (acc[x, col, n] + total).astype(jnp.bfloat16)
        else:
            rest[int(x > 0), col, n] = acc[x, col, n] + total

    copies = []
    for x in (1, 2, 0, 3):
        for col in range(2):
            first = (SIDE_LOW, SIDE_HIGH)[col]
            pieces = [
                (first + near, block_from(mids[col], near - 1))
                for near in (x - 1, x, x + 1)
                if 0 < near < cells_x - 1
            ]
            accumulate(table_m, table_q, own, x, col, pieces, write, 6)
            if 0 < x < cells_x - 1:
                copies.append(pltpu.make_async_copy(held.at[x - 1, col], out.at[x, col], sems.at[x - 1, col]))
                copies[-1].start()
    for copy in copies:
        copy.wait()


def edge_kernel(table_m, table_q, own, rest, near_low, near_high, wrap, begun, out, held, sems):
    cells_x = own.shape[0]

    def write(x, col, n, total):
        at = int(x > 0)
        held[at, col, n] = (rest[at, col, n] + total).astype(jnp.bfloat16)

    copies = []
    for at, x in enumerate((0, cells_x - 1)):
        first, near = ((NEAR_LOW, near_low), (NEAR_HIGH, near_high))[at]
        for col in range(2):
            pieces = [(first + y, block_from(near, y)) for y in range(4)]
            pieces += [(WRAP + y, block_from(wrap, y)) for y in range(2)]
            accumulate(table_m, table_q, own, x, col, pieces, write, 6)
            copies.append(pltpu.make_async_copy(held.at[at, col], out.at[x, col], sems.at[at, col]))
            copies[-1].start()
    for copy in copies:
        copy.wait()


def run_kernel(body, tables, own, sites, flops, begun=None, middle=False):
    whole, half = ((count, 2) + BLOCKS for count in (own.shape[0], 2))
    in_vmem, in_hbm = pl.BlockSpec(memory_space=pltpu.VMEM), pl.BlockSpec(memory_space=pl.ANY)
    out_shape, out_specs = jax.ShapeDtypeStruct(whole, jnp.float32), in_vmem
    in_specs = [pl.BlockSpec(memory_space=pltpu.SMEM)] * 2 + [in_vmem] * (1 + len(sites))
    held, aliases = [], {}
    if middle or begun is not None:
        out_shape, out_specs = jax.ShapeDtypeStruct(whole, jnp.bfloat16), in_hbm
        held = [pltpu.VMEM(half, jnp.bfloat16), pltpu.SemaphoreType.DMA((2, 2))]
    if middle:
        out_shape, out_specs = (out_shape, jax.ShapeDtypeStruct(half, jnp.float32)), (out_specs, in_vmem)
    if begun is not None:
        aliases = {len(in_specs): 0}
        in_specs, sites = in_specs + [in_hbm], [*sites, begun]
    return pl.pallas_call(
        body,
        out_shape=out_shape,
        in_specs=in_specs,
        out_specs=out_specs,
        scratch_shapes=held,
        input_output_aliases=aliases,
        compiler_params=pltpu.CompilerParams(vmem_limit_bytes=32 * 2**20),
        cost_estimate=pl.CostEstimate(flops=flops, bytes_accessed=2**10, transcendentals=0),
    )(*tables, own, *sites)


def make_tables(p_cols, c_cols, cells_x, cells_y):
    total_x, total_y, blocks = p_cols.shape
    at_blk, at_row = lax.axis_index("blk"), lax.axis_index("rows")
    first, last = at_blk == 0, at_blk == lax.axis_size("blk") - 1
    near = [(x, y) for x in range(cells_x) for y in range(cells_y)]
    wide = [-1] * 4 + [cells_x] * 4
    sides, side_y = list(range(cells_x)) * 2, [-1] * cells_x + [cells_y] * cells_x
    dx = [x for x, _ in near] + sides + wide + [0, 0]
    plain = [y for _, y in near] + side_y + [0, 1, -1, 2] * 2 + [2, 1]
    turned = [y for _, y in near] + side_y + [-2, -1, -3, 0] * 2 + [2, 1]
    dx, plain, turned = (np.array(v, np.int32) for v in (dx, plain, turned))
    is_wrap = np.arange(PIECES) >= WRAP
    dx = jnp.where(is_wrap, jnp.where(first, -1, cells_x), dx)
    swapped = ((dx < 0) & first) | ((dx >= cells_x) & last)
    dy = jnp.where(swapped, turned, plain)
    site_x = (at_blk * cells_x + dx + total_x) % total_x
    site_y = (at_row * cells_y + dy + total_y) % total_y
    ids = site_x * total_y + site_y
    cols = p_cols.reshape(total_x * total_y, blocks)[ids]
    ids = jnp.where(is_wrap & ~(first | last), -1, ids)
    own = cols[: cells_x * cells_y]
    slots = jnp.arange(blocks, dtype=jnp.int32)
    is_left = own[:, None, :] == ids[None, :, None]
    table_m = jnp.sum(jnp.where(is_left, slots, 0), axis=2)
    has_left = jnp.any(is_left, axis=2)
    targets = c_cols.reshape(cells_x * cells_y, -1)
    is_right = (cols[None, :, None, :] == targets[:, None, :, None]) & has_left[:, :, None, None]
    table_q = 8 + jnp.sum(jnp.where(is_right, slots - 8, 0), axis=3)
    return table_m.reshape(-1).astype(jnp.int32), table_q.reshape(-1).astype(jnp.int32)


def on_device(p_vals, p_cols, c_cols):
    cells_x, cells_y = p_vals.shape[:2]
    n_blk, n_rows = lax.axis_size("blk"), lax.axis_size("rows")
    last = cells_x - 1
    first = lax.axis_index("blk") == 0
    along_y = lambda value, shift: send(value, moves_y(shift, n_blk, n_rows), n_rows)
    along_x = lambda value, shift: send(value, moves_x(shift, n_blk, n_rows), n_rows)
    past_edge = lambda value: send(value, moves_wrap(n_blk, n_rows), n_rows)
    tie = lax.optimization_barrier

    rim_low = along_y(jnp.stack([p_vals[0, 1], p_vals[last, 1]]), 1)
    rim_high = along_y(jnp.stack([p_vals[0, 0], p_vals[last, 0]]), -1)

    tables = make_tables(p_cols, c_cols, cells_x, cells_y)
    tables, middle = tie((tables, (p_vals[1:last, 1], p_vals[1:last, 0])))
    acc = run_kernel(column_kernel, tables, p_vals, [], 4 * 10**9)
    mid_low = along_y(middle[0], 1)
    mid_high = along_y(middle[1], -1)

    acc = run_kernel(own_kernel, tables, p_vals, [acc], 4 * 10**9)
    acc, rim_low, rim_high = tie((acc, rim_low, rim_high))
    below = jnp.stack([p_vals[0, 0], p_vals[0, 1], rim_low[0], rim_high[0]])
    above = jnp.stack([p_vals[last, 0], p_vals[last, 1], rim_low[1], rim_high[1]])
    pair = jnp.where(first, below[0:3:2], above[0:3:2])
    near = [along_x(above, 1), along_x(below, -1), past_edge(pair)]

    acc = run_kernel(rim_kernel, tables, p_vals, [acc, rim_low, rim_high], 10**6)
    begun, rest = run_kernel(middle_kernel, tables, p_vals, [acc, mid_low, mid_high], 5 * 10**10, middle=True)
    return run_kernel(edge_kernel, tables, p_vals, [rest, *near], 10**6, begun=begun)


def solution(mesh):
    placed = (P("blk", "rows", None, None, None), P(), P("blk", "rows", None))
    return jax.shard_map(
        on_device,
        mesh=mesh,
        in_specs=placed,
        out_specs=P("blk", "rows", None, None, None),
        check_vma=False,
    )
```
